256 devices in a mesh: pipe: 16 (over y_lo, x, core), tensor: 16 (over y_hi, z).
Axes of the slice: x: 4, y: 4 (y_hi: 2, y_lo: 2; y = y_hi * 2 + y_lo), z: 8, core: 2. Of those that a mesh axis runs over, the one named last changes fastest.
Arguments:
- new_inputs: bfloat16 [1, 128, 6144], P(None, 'tensor'), may hold values from -6 to 6
- new_grads: bfloat16 [1, 128, 6144], P(None, 'tensor'), may hold values from -6 to 6
- forward_state: bfloat16 [16, 128, 6144], P('pipe', 'tensor'), may hold values from -6 to 6
- backward_state: bfloat16 [16, 128, 6144], P('pipe', 'tensor'), may hold values from -6 to 6
- stashed: bfloat16 [16, 2, 128, 6144], P('pipe', None, 'tensor'), may hold values from -6 to 6
- new_docs: int32 [1, 128], replicated, may hold values from 0 to 3, never falling along the last dimension, each value on 1 to 64 neighbouring positions
- state_docs: int32 [16, 128], P('pipe'), may hold values from 0 to 3, never falling along the last dimension, each value on 1 to 64 neighbouring positions
- stash_docs: int32 [16, 2, 128], P('pipe'), may hold values from 0 to 3, never falling along the last dimension, each value on 1 to 64 neighbouring positions
- stash_order: int32 [16, 2], P('pipe'), may hold values from 0 to 1, each once within a row
- norm_gain: float32 [16, 6144], P('pipe'), may hold values from 0.1 to 1.9
- qkv_weight: bfloat16 [16, 6144, 3, 4096], P('pipe', None, None, 'tensor'), may hold values from -0.26791294 to 0.26791294
- out_weight: bfloat16 [16, 4096, 6144], P('pipe', 'tensor'), may hold values from -0.25 to 0.25
Outputs:
- forward_out: bfloat16 [16, 128, 6144], P('pipe', 'tensor')
- backward_out: bfloat16 [16, 128, 6144], P('pipe', 'tensor')
The draws below stay inside these ranges and needn't reach their ends.
Inputs may be any that keep to these rules, and one draw needn't show every extreme that they name: Each row of stash_order names each of the 2 stashed micro-batches of its section once. `new_docs`: ids never fall along a row; each document holds 1 to 64 tokens and one of each row exactly 64. `state_docs`: as for new_docs. `stash_docs`: as for new_docs.
All inputs are finite; a program needn't handle non-finite values.
Results may differ from the reference program's by a relative error of at most 0.035.
The reference program's roundings to bfloat16 on the way count: a program that leaves them out, or rounds other values in their place, can miss the bound.
Values may be sent and summed in bfloat16 or wider, within the bound.
No kernel may reach another device: no remote copies, remote signals or barrier semaphores. Data moves between devices by JAX's collectives and lax.ppermute only.
A program may use at most 128 MiB of HBM per device.

```python
import math
import jax
import jax.numpy as jnp
import numpy as np
from jax import lax

D = 6144
HD = 128
SEQ = 128
STEPS = 2
DOCS = 4
LAYERS = 16
HEADS = 32
INNER = 4096


def draw_qkv_weight(key, part):
    key = jax.random.fold_in(key, 7)
    key_base = jax.random.fold_in(key, 0)
    base = jnp.clip(jax.random.normal(key_base, (LAYERS, D, 3, INNER), jnp.float32), -4.0, 4.0)
    return (base * D ** (-0.5)).astype(jnp.bfloat16)


def block_levels(own_key, extent, cuts, smallest, largest):
    loudness, own = 1.0, jax.random.fold_in(own_key, 6)
    for position, parts in cuts:
        draws = jnp.exp(jax.random.uniform(jax.random.fold_in(own, position), (parts,), jnp.float32, smallest / len(cuts), largest / len(cuts)))
        loudness = loudness * jnp.repeat(draws, extent[position] // parts).reshape([-1 if axis == position else 1 for axis in range(len(extent))])
    return loudness


def split_up(number_of, total, limit, slope):
    weights = [(1 << 20) // math.isqrt(grade ** slope) + 1 for grade in range(2, number_of + 1)]
    spare, holding = total - limit - (number_of - 1), [1] * (number_of - 1)
    while spare > 0:
        free = [i for i in range(number_of - 1) if holding[i] < limit]
        pool, remaining = sum([weights[i] for i in free]), spare
        for i in free:
            more = min(limit - holding[i], max(1, remaining * weights[i] // pool), spare)
            holding[i] = holding[i] + more
            spare = spare - more
    return np.array([limit] + holding)


def ragged_sizes(key, amount, total, limit, lean):
    if amount == 2:
        one = jax.random.randint(key, (), max(1, total - limit), min(limit, total - 1) + 1)
        return jnp.stack([one, total - one])
    tallies = jnp.asarray(split_up(amount, total, limit, lean), jnp.int32)
    couples = (amount - 1) // 2
    giver, sink = tallies[1:1 + 2 * couples:2], tallies[2:2 + 2 * couples:2]
    slack = jnp.minimum(giver - 1, limit - sink)
    moved = jax.random.randint(jax.random.fold_in(key, 1), (couples,), 0, 1 << 20) % (slack + 1)
    tallies = tallies.at[1:1 + 2 * couples:2].set(giver - moved).at[2:2 + 2 * couples:2].set(sink + moved)
    return tallies[jax.random.permutation(jax.random.fold_in(key, 2), amount)]


def centred(stream_key, extent, width, most, shards=(), kind=jnp.bfloat16):
    drawn = jax.random.normal(stream_key, extent, jnp.float32) * width
    if len(shards) > 0:
        drawn = block_levels(stream_key, extent, shards, -0.22, 0.18) * drawn
    return jnp.clip(drawn, min=-most, max=most).astype(kind)


def setup_inputs(seed: int = 0) -> dict:
    seeds = jax.random.split(jax.random.key(seed), 13)
    return {
        "new_inputs": centred(seeds[0], (STEPS - 1, SEQ, D), 1.0, 6.0, ((1, 16),)),
        "new_grads": centred(seeds[1], (STEPS - 1, SEQ, D), 1.0, 6.0, ((1, 16),)),
        "forward_state": centred(seeds[2], (LAYERS, SEQ, D), 1.0, 6.0, ((0, 16), (1, 16))),
        "backward_state": centred(seeds[3], (LAYERS, SEQ, D), 1.0, 6.0, ((0, 16), (1, 16))),
        "stashed": centred(seeds[4], (LAYERS, STEPS, SEQ, D), 1.0, 6.0, ((0, 16), (2, 16))),
        "new_docs": jax.vmap(lambda own: jnp.searchsorted(jnp.cumsum(ragged_sizes(own, DOCS, SEQ, SEQ // 2, 0)), jnp.arange(SEQ), side="right"))(jax.random.split(seeds[5], (STEPS - 1))).reshape((STEPS - 1, SEQ)).astype(jnp.int32),
        "state_docs": jax.vmap(lambda own: jnp.searchsorted(jnp.cumsum(ragged_sizes(own, DOCS, SEQ, SEQ // 2, 0)), jnp.arange(SEQ), side="right"))(jax.random.split(seeds[6], LAYERS)).reshape((LAYERS, SEQ)).astype(jnp.int32),
        "stash_docs": jax.vmap(lambda own: jnp.searchsorted(jnp.cumsum(ragged_sizes(own, DOCS, SEQ, SEQ // 2, 0)), jnp.arange(SEQ), side="right"))(jax.random.split(seeds[7], LAYERS * STEPS)).reshape((LAYERS, STEPS, SEQ)).astype(jnp.int32),
        "stash_order": jax.vmap(lambda own: jax.random.permutation(own, STEPS))(jax.random.split(seeds[8], LAYERS)).reshape((LAYERS, STEPS)).astype(jnp.int32),
        "norm_gain": jnp.clip(1.0 + 0.18 * jax.random.normal(seeds[9], (LAYERS, D), jnp.float32), 0.1, 1.9),
        "qkv_weight": draw_qkv_weight(jax.random.fold_in(seeds[12], 71), 0),
        "out_weight": centred(seeds[11], (LAYERS, INNER, D), (INNER // 8) ** -0.5, 0.25, ((0, 16), (1, 16))),
    }


NORM_EPS = 1e-05

def normalize(row_block, norm_gain):
    values = row_block.astype(jnp.float32)
    centered = values - lax.optimization_barrier(jnp.mean(values, axis=-1, keepdims=True))
    inv_scale = lax.rsqrt(lax.optimization_barrier(jnp.mean(centered * centered, axis=-1, keepdims=True)) + NORM_EPS)
    scaled = centered * inv_scale
    return (scaled * norm_gain, scaled, inv_scale)

def split_heads(qkv_rows):
    grouped = qkv_rows.reshape(qkv_rows.shape[0], 3, -1, HD).astype(jnp.float32)
    return (grouped[:, 0], grouped[:, 1], grouped[:, 2])

def soft_weights(query_rows, key_rows, doc_ids):
    scores = jnp.einsum('qhd,khd->hqk', query_rows, key_rows) / math.sqrt(HD)
    positions = lax.iota(jnp.int32, query_rows.shape[0])
    visible = (doc_ids[:, None] == doc_ids[None, :]) & (positions[:, None] >= positions[None, :])
    scores = jnp.where(visible[None], scores, -jnp.inf)
    shifted = jnp.exp(scores - lax.optimization_barrier(jnp.max(scores, axis=-1, keepdims=True)))
    return shifted / lax.optimization_barrier(jnp.sum(shifted, axis=-1, keepdims=True))

def layer_forward(row_block, doc_ids, norm_gain, qkv_weight, out_weight):
    normed = normalize(row_block, norm_gain)[0].astype(jnp.bfloat16)
    qkv_rows = jnp.dot(normed, qkv_weight.reshape(D, 3 * INNER), preferred_element_type=jnp.float32).astype(jnp.bfloat16)
    query_rows, key_rows, value_rows = split_heads(qkv_rows)
    soft_half = soft_weights(query_rows, key_rows, doc_ids).astype(jnp.bfloat16)
    mixed_heads = jnp.einsum('hqk,khd->qhd', soft_half.astype(jnp.float32), value_rows).astype(jnp.bfloat16)
    mixed_heads = mixed_heads.reshape(SEQ, INNER)
    projected = jnp.dot(mixed_heads, out_weight, preferred_element_type=jnp.float32)
    return (row_block.astype(jnp.float32) + projected).astype(jnp.bfloat16)

def layer_backward(row_block, doc_ids, grad_rows, norm_gain, qkv_weight, out_weight):
    flat_weight = qkv_weight.reshape(D, 3 * INNER)
    normed = normalize(row_block, norm_gain)[0].astype(jnp.bfloat16)
    qkv_rows = jnp.dot(normed, flat_weight, preferred_element_type=jnp.float32).astype(jnp.bfloat16)
    query_rows, key_rows, value_rows = split_heads(qkv_rows)
    soft_probs = soft_weights(query_rows, key_rows, doc_ids)
    soft_half = soft_probs.astype(jnp.bfloat16).astype(jnp.float32)
    d_mixed = jnp.dot(grad_rows, out_weight.T, preferred_element_type=jnp.float32).astype(jnp.bfloat16)
    d_mixed = d_mixed.reshape(SEQ, HEADS, HD).astype(jnp.float32)
    d_soft = jnp.einsum('qhd,khd->hqk', d_mixed, value_rows)
    d_value = jnp.einsum('hqk,qhd->khd', soft_half, d_mixed).astype(jnp.bfloat16)
    d_scores = soft_probs * (d_soft - lax.optimization_barrier(jnp.sum(d_soft * soft_probs, axis=-1, keepdims=True))) / math.sqrt(HD)
    d_scores = d_scores.astype(jnp.bfloat16).astype(jnp.float32)
    d_query = jnp.einsum('hqk,khd->qhd', d_scores, key_rows).astype(jnp.bfloat16)
    d_key = jnp.einsum('hqk,qhd->khd', d_scores, query_rows).astype(jnp.bfloat16)
    d_qkv = jnp.stack([d_query, d_key, d_value], axis=1).reshape(SEQ, 3 * INNER)
    d_normed = jnp.dot(d_qkv, flat_weight.T, preferred_element_type=jnp.float32)
    discarded, scaled, inv_scale = normalize(row_block, norm_gain)
    d_scaled = d_normed * norm_gain
    d_rows = inv_scale * (d_scaled - lax.optimization_barrier(jnp.mean(d_scaled, axis=-1, keepdims=True)) - scaled * lax.optimization_barrier(jnp.mean(d_scaled * scaled, axis=-1, keepdims=True)))
    return (grad_rows.astype(jnp.float32) + d_rows).astype(jnp.bfloat16)

def reference(new_inputs, new_grads, forward_state, backward_state, stashed, new_docs, state_docs, stash_docs, stash_order, norm_gain, qkv_weight, out_weight):
    forward_now = forward_state
    docs_now = state_docs
    backward_now = backward_state
    forward_next = forward_state
    backward_next = backward_state
    for phase in range(STEPS):
        outputs = []
        gradients = []
        for section in range(LAYERS):
            outputs.append(layer_forward(forward_now[section], docs_now[section], norm_gain[section], qkv_weight[section], out_weight[section]))
            stash_slot = stash_order[section, phase].astype(jnp.int32)
            stored = lax.dynamic_index_in_dim(stashed[section], stash_slot, 0, keepdims=False)
            stored_ids = lax.dynamic_index_in_dim(stash_docs[section], stash_slot, 0, keepdims=False)
            gradients.append(layer_backward(stored, stored_ids, backward_now[section], norm_gain[section], qkv_weight[section], out_weight[section]))
        forward_next = jnp.stack(outputs)
        backward_next = jnp.stack(gradients)
        if phase + 1 < STEPS:
            forward_now = jnp.concatenate([new_inputs[phase][None], forward_next[:-1]], axis=0)
            docs_now = jnp.concatenate([new_docs[phase][None], docs_now[:-1]], axis=0)
            backward_now = jnp.concatenate([backward_next[1:], new_grads[phase][None]], axis=0)
    return (forward_next, backward_next)
```

```python
import math

import jax
import jax.numpy as jnp
from jax import lax
from jax.sharding import PartitionSpec as P

HD = 128
STEPS = 2
NORM_EPS = 1e-05
TRANSPOSED = (((1,), (1,)), ((), ()))
YS, ZS = 2, 8
Z_ORDER = (0, 1, -3, -1, 3, 2, -2, 4)


def from_behind(value, axis, steps):
    count = lax.axis_size(axis)
    first, last = (max(0, -steps), min(count, count - steps))
    return lax.ppermute(value, axis, [(source, source + steps) for source in range(first, last)])


def z_shift(value, steps):
    pairs = [(a * ZS + b, a * ZS + (b + steps) % ZS) for a in range(YS) for b in range(ZS)]
    return lax.ppermute(value, "tensor", pairs)


def y_swap(value):
    pairs = [(a * ZS + b, (1 - a) * ZS + b) for a in range(YS) for b in range(ZS)]
    return lax.ppermute(value, "tensor", pairs)


def ring(piece):
    held = {0: piece}
    ahead = behind = piece
    for hop in range(1, 5):
        ahead = z_shift(ahead, 1)
        held[-hop if hop < 4 else 4] = ahead
        if hop < 4:
            behind = z_shift(behind, -1)
            held[hop] = behind
    return held


def gather_z_first(piece):
    held = ring(piece)
    early, late = ((0, 1, -1, 2, -2), (-3, 3, 4))
    size = piece.shape[0]
    other = {}
    for group in (early, late):
        swapped = y_swap(jnp.concatenate([held[z] for z in group], axis=0))
        for place, z in enumerate(group):
            other[z] = swapped[place * size : (place + 1) * size]
    return jnp.concatenate([held[z] for z in Z_ORDER] + [other[z] for z in Z_ORDER], axis=0)


def gather_y_first(piece):
    size = piece.shape[0]
    held = ring(jnp.concatenate([piece, y_swap(piece)], axis=0))
    return jnp.concatenate(
        [held[z][:size] for z in Z_ORDER] + [held[z][size:] for z in Z_ORDER], axis=0
    )


def scatter_sum(partial):
    half = partial.shape[0] // 2
    size = half // ZS
    got = y_swap(partial[half:].astype(jnp.bfloat16))
    rows = partial[:half] + got.astype(jnp.float32)
    sent = rows.astype(jnp.bfloat16)
    up = z_shift(sent[size : 3 * size], 1).astype(jnp.float32)
    down = z_shift(sent[3 * size : 5 * size], -1).astype(jnp.float32)
    up_two = z_shift(sent[5 * size : 6 * size], 2).astype(jnp.float32)
    down_two = z_shift(sent[6 * size : 7 * size], -2).astype(jnp.float32)
    far = z_shift((rows[7 * size :] + up[size:] + down[size:]).astype(jnp.bfloat16), 4)
    return rows[:size] + up[:size] + down[:size] + up_two + down_two + far.astype(jnp.float32)


def normalize(row_block, norm_gain):
    values = row_block.astype(jnp.float32)
    centered = values - jnp.mean(values, axis=-1, keepdims=True)
    inv_scale = lax.rsqrt(jnp.mean(centered * centered, axis=-1, keepdims=True) + NORM_EPS)
    scaled = centered * inv_scale
    return (scaled * norm_gain, scaled, inv_scale)


def split_heads(qkv_rows, head_size):
    grouped = qkv_rows.reshape(qkv_rows.shape[0], 3, -1, head_size)
    return (grouped[:, 0], grouped[:, 1], grouped[:, 2])


def soft_weights(query_rows, key_rows, doc_ids, positions):
    scores = jnp.einsum(
        "qhd,khd->hqk", query_rows, key_rows, preferred_element_type=jnp.float32
    ) / math.sqrt(query_rows.shape[2])
    visible = (doc_ids[:, None] == doc_ids[None, :]) & (positions[:, None] >= positions[None, :])
    scores = jnp.where(visible[None], scores, -jnp.inf)
    shifted = jnp.exp(scores - jnp.max(scores, axis=-1, keepdims=True))
    return shifted / jnp.sum(shifted, axis=-1, keepdims=True)


def attend(qkv_rows, doc_ids, positions, head_size):
    query_rows, key_rows, value_rows = split_heads(qkv_rows, head_size)
    soft_half = soft_weights(query_rows, key_rows, doc_ids, positions).astype(jnp.bfloat16)
    mixed_heads = jnp.einsum(
        "hqk,khd->qhd", soft_half, value_rows, preferred_element_type=jnp.float32
    ).astype(jnp.bfloat16)
    return mixed_heads.reshape(qkv_rows.shape[0], -1)


def attend_backward(qkv_rows, grad_full, doc_ids, positions, proj_weight, head_size):
    query_rows, key_rows, value_rows = split_heads(qkv_rows, head_size)
    soft_probs = soft_weights(query_rows, key_rows, doc_ids, positions)
    soft_half = soft_probs.astype(jnp.bfloat16)
    d_mixed = lax.dot_general(
        grad_full, proj_weight, TRANSPOSED, preferred_element_type=jnp.float32
    )
    d_mixed = d_mixed.astype(jnp.bfloat16).reshape(query_rows.shape)
    d_soft = jnp.einsum("qhd,khd->hqk", d_mixed, value_rows, preferred_element_type=jnp.float32)
    d_value = jnp.einsum(
        "hqk,qhd->khd", soft_half, d_mixed, preferred_element_type=jnp.float32
    ).astype(jnp.bfloat16)
    d_scores = (
        soft_probs
        * (d_soft - jnp.sum(d_soft * soft_probs, axis=-1, keepdims=True))
        / math.sqrt(head_size)
    )
    d_scores = d_scores.astype(jnp.bfloat16)
    d_query = jnp.einsum(
        "hqk,khd->qhd", d_scores, key_rows, preferred_element_type=jnp.float32
    ).astype(jnp.bfloat16)
    d_key = jnp.einsum(
        "hqk,qhd->khd", d_scores, query_rows, preferred_element_type=jnp.float32
    ).astype(jnp.bfloat16)
    return jnp.stack([d_query, d_key, d_value], axis=1).reshape(qkv_rows.shape[0], -1)


def norm_backward(row_block, grad_rows, d_normed, norm_gain):
    discarded, scaled, inv_scale = normalize(row_block, norm_gain)
    d_scaled = d_normed * norm_gain
    d_rows = inv_scale * (
        d_scaled
        - jnp.mean(d_scaled, axis=-1, keepdims=True)
        - scaled * jnp.mean(d_scaled * scaled, axis=-1, keepdims=True)
    )
    return (grad_rows.astype(jnp.float32) + d_rows).astype(jnp.bfloat16)


def on_device(
    new_inputs,
    new_grads,
    forward_state,
    backward_state,
    stashed,
    new_docs,
    state_docs,
    stash_docs,
    stash_order,
    norm_gain,
    qkv_weight,
    out_weight,
):
    head_size = HD
    gain_row = norm_gain[0]
    model_dim = qkv_weight.shape[1]
    flat_weight = qkv_weight[0].reshape(model_dim, -1)
    proj_weight = out_weight[0]
    pipe_index = lax.axis_index("pipe")
    last_pipe = lax.axis_size("pipe") - 1
    tensor_index = lax.axis_index("tensor")
    y_index, z_index = tensor_index // ZS, tensor_index % ZS
    size = forward_state.shape[1]
    tokens = size * YS * ZS
    positions = jnp.concatenate(
        [
            ((y_index + y) % YS * ZS + (z_index + z + ZS) % ZS) * size + lax.iota(jnp.int32, size)
            for y in range(YS)
            for z in Z_ORDER
        ]
    )
    chosen = positions[:, None] == lax.iota(jnp.int32, tokens)[None, :]

    def in_order(ids):
        return jnp.sum(jnp.where(chosen, ids[None, :], 0), axis=1)

    forward_now = forward_state[0]
    backward_now = backward_state[0]
    docs_now = state_docs[0]
    moved_docs = from_behind(docs_now, "pipe", 1)
    docs_by_step = [docs_now, jnp.where(pipe_index == 0, new_docs[0], moved_docs)]
    stored_by_step, stored_ids_by_step = [], []
    for phase in range(STEPS):
        stash_slot = stash_order[0, phase]
        stored_by_step.append(lax.dynamic_index_in_dim(stashed[0], stash_slot, 0, keepdims=False))
        stored_ids_by_step.append(
            lax.dynamic_index_in_dim(stash_docs[0], stash_slot, 0, keepdims=False)
        )
    forward_next = forward_now
    backward_next = backward_now
    for phase in range(STEPS):
        stored = stored_by_step[phase]
        normed_stash = normalize(stored, gain_row)[0].astype(jnp.bfloat16)
        normed = normalize(forward_now, gain_row)[0].astype(jnp.bfloat16)
        if phase == 0:
            stash_whole = gather_y_first(normed_stash)
        else:
            stash_whole = lax.all_gather(normed_stash, "tensor", axis=0, tiled=True)
        qkv_stash = jnp.dot(stash_whole, flat_weight, preferred_element_type=jnp.float32).astype(
            jnp.bfloat16
        )
        if phase > 0:
            qkv_stash = jnp.dot(
                chosen.astype(jnp.bfloat16), qkv_stash, preferred_element_type=jnp.float32
            ).astype(jnp.bfloat16)
        grad_whole = gather_z_first(backward_now)
        normed_whole = gather_z_first(normed)
        qkv_rows = jnp.dot(
            normed_whole, flat_weight, preferred_element_type=jnp.float32
        ).astype(jnp.bfloat16)
        mixed_heads = attend(qkv_rows, in_order(docs_by_step[phase]), positions, head_size)
        attn_total = scatter_sum(
            jnp.dot(mixed_heads, proj_weight, preferred_element_type=jnp.float32)
        )
        forward_next = (forward_now.astype(jnp.float32) + attn_total).astype(jnp.bfloat16)
        d_qkv = attend_backward(
            qkv_stash,
            grad_whole,
            in_order(stored_ids_by_step[phase]),
            positions,
            proj_weight,
            head_size,
        )
        d_normed = scatter_sum(
            lax.dot_general(d_qkv, flat_weight, TRANSPOSED, preferred_element_type=jnp.float32)
        )
        backward_next = norm_backward(stored, backward_now, d_normed, gain_row)
        if phase + 1 < STEPS:
            moved_rows = from_behind(forward_next, "pipe", 1)
            forward_now = jnp.where(pipe_index == 0, new_inputs[phase], moved_rows)
            moved_grads = from_behind(backward_next, "pipe", -1)
            backward_now = jnp.where(pipe_index == last_pipe, new_grads[phase], moved_grads)
    return (forward_next[None], backward_next[None])


def solution(mesh):
    return jax.shard_map(
        on_device,
        mesh=mesh,
        in_specs=(
            P(None, "tensor", None),
            P(None, "tensor", None),
            P("pipe", "tensor", None),
            P("pipe", "tensor", None),
            P("pipe", None, "tensor", None),
            P(),
            P("pipe", None),
            P("pipe", None, None),
            P("pipe", None),
            P("pipe", None),
            P("pipe", None, None, "tensor"),
            P("pipe", "tensor", None),
        ),
        out_specs=(P("pipe", "tensor", None), P("pipe", "tensor", None)),
        check_vma=False,
    )
```

```python
import functools
import math

import jax
import jax.numpy as jnp
from jax import lax
from jax.experimental import pallas as pl
from jax.experimental.pallas import tpu as pltpu
from jax.sharding import Mesh
from jax.sharding import PartitionSpec as P

HD = 128
STEPS = 2
NORM_EPS = 1e-05
TRANSPOSED = (((1,), (1,)), ((), ()))
YS, ZS = 2, 8
Z_ORDER = (0, 1, -3, -1, 3, 2, -2, 4)
EARLY, LATE = (0, 1, -1, 2, -2), (-3, 3, 4)
BF16, F32 = jnp.bfloat16, jnp.float32
VMEM_LIMIT = 48 * 1024 * 1024


def from_behind(value, steps):
    count = lax.axis_size("pipe")
    first, last = (max(0, -steps), min(count, count - steps))
    return lax.ppermute(value, "pipe", [(source, source + steps) for source in range(first, last)])


def from_behind_swapped(value, steps):
    count = lax.axis_size("pipe")
    first, last = (max(0, -steps), min(count, count - steps))
    pairs = [
        (s * YS + y, (s + steps) * YS + 1 - y) for s in range(first, last) for y in range(YS)
    ]
    return lax.ppermute(value, ("pipe", "y"), pairs)


def y_swap(value):
    return lax.ppermute(value, "y", [(0, 1), (1, 0)])


def after(value, *others):
    return lax.optimization_barrier((value, *others))[0]


def z_shift(value, steps):
    return lax.ppermute(value, "z", [(z, (z + steps) % ZS) for z in range(ZS)])


def ring(piece, between=None):
    held = {0: piece}
    ahead = behind = piece
    for hop in range(1, 5):
        if hop == 2 and between is not None:
            ready = between(ahead)
            ahead, behind = after(ahead, ready), after(behind, ready)
        ahead = z_shift(ahead, 1)
        held[-hop if hop < 4 else 4] = ahead
        if hop < 4:
            behind = z_shift(behind, -1)
            held[hop] = behind
    return held


def gather_z_first(piece, between=None):
    held = ring(piece, between)
    parts = [y_swap(stack_rows(*[held[z] for z in group])) for group in (EARLY, LATE)]
    return [held[z] for z in EARLY + LATE] + parts


def gather_y_first(piece):
    held = ring(piece)
    return [held[z] for z in Z_ORDER]


def exchange(rows):
    return lax.all_to_all(rows, "z", 0, 0, tiled=True)


def call(kernel, out_shape, flops=0, moved=0, **options):
    if flops:
        options["cost_estimate"] = pl.CostEstimate(
            flops=flops, bytes_accessed=moved, transcendentals=0
        )
    return pl.pallas_call(
        kernel,
        out_shape=out_shape,
        compiler_params=pltpu.CompilerParams(vmem_limit_bytes=VMEM_LIMIT),
        **options,
    )


def shaped(shape, dtype):
    return jax.ShapeDtypeStruct(shape, dtype)


def normalize(values, gain):
    centered = values - jnp.mean(values, axis=-1, keepdims=True)
    inv_scale = lax.rsqrt(jnp.mean(centered * centered, axis=-1, keepdims=True) + NORM_EPS)
    scaled = centered * inv_scale
    return (scaled * gain, scaled, inv_scale)


def normalized(ref, gain_ref):
    return normalize(ref[...].astype(F32), gain_ref[...])[0]


def normalize_kernel(a_ref, b_ref, gain_ref, out_ref):
    rows = [normalized(a_ref, gain_ref), normalized(b_ref, gain_ref)]
    out_ref[...] = jnp.concatenate(rows, axis=0).astype(BF16)


def normalize_rows(a, b, gain):
    shape = shaped((2 * a.shape[0], a.shape[1]), BF16)
    return call(normalize_kernel, shape)(a, b, gain)


def start_kernel(rows_ref, gain_ref, out_ref):
    out_ref[...] = normalized(rows_ref, gain_ref).astype(BF16)


def stash_kernel(order_ref, own_ref, other_ref, gain_ref, *out_refs):
    for step, out_ref in enumerate(out_refs):
        slot = order_ref[0, step]
        rows = [normalized(ref.at[slot], gain_ref) for ref in (own_ref, other_ref)]
        out_ref[...] = jnp.concatenate(rows, axis=0).astype(BF16)


def stash_rows(order, own, other, gain):
    steps, size, width = own.shape
    in_vmem = pl.BlockSpec(memory_space=pltpu.VMEM)
    return call(
        stash_kernel,
        [shaped((YS * size, width), BF16)] * steps,
        in_specs=[pl.BlockSpec(memory_space=pltpu.SMEM)] + [in_vmem] * 3,
    )(order, own, other, gain)


def stack_kernel(*refs):
    *piece_refs, out_ref = refs
    rows = [ref[...].astype(F32) for ref in piece_refs]
    out_ref[...] = jnp.concatenate(rows, axis=0).astype(BF16)


def stack_rows(*pieces):
    tokens = sum(piece.shape[0] for piece in pieces)
    return call(stack_kernel, shaped((tokens, pieces[0].shape[1]), BF16))(*pieces)


def split_kernel(size, own_ref, got_ref, keep_ref, up_ref, down_ref, up_two_ref, down_two_ref, far_ref):
    rows = own_ref[...].astype(F32) + got_ref[...].astype(F32)
    keep_ref[...] = rows[:size]
    up_ref[...] = rows[size : 3 * size].astype(BF16)
    down_ref[...] = rows[3 * size : 5 * size].astype(BF16)
    up_two_ref[...] = rows[5 * size : 6 * size].astype(BF16)
    down_two_ref[...] = rows[6 * size : 7 * size].astype(BF16)
    far_ref[...] = rows[7 * size :]


def far_kernel(size, far_ref, up_ref, down_ref, out_ref):
    up, down = up_ref[...].astype(F32), down_ref[...].astype(F32)
    out_ref[...] = (far_ref[...] + up[size:] + down[size:]).astype(BF16)


def scatter_sum(own, got):
    half, width = own.shape
    size, block = half // ZS, width // 3
    outs = [(size, F32), (2 * size, BF16), (2 * size, BF16), (size, BF16), (size, BF16), (size, F32)]
    column = lambda tokens: pl.BlockSpec((tokens, block), lambda i: (0, i))
    keep, up, down, up_two, down_two, far = call(
        functools.partial(split_kernel, size),
        [shaped((tokens, width), dtype) for tokens, dtype in outs],
        grid=(width // block,),
        in_specs=[column(half), column(half)],
        out_specs=[column(tokens) for tokens, _ in outs],
    )(own, got)
    up, down = z_shift(up, 1), z_shift(down, -1)
    up_two, down_two = z_shift(up_two, 2), z_shift(down_two, -2)
    far = call(functools.partial(far_kernel, size), shaped((size, width), BF16))(far, up, down)
    return (keep, up, down, up_two, down_two, z_shift(far, 4))


def total(keep_ref, up_ref, down_ref, up_two_ref, down_two_ref, far_ref):
    size = keep_ref.shape[0]
    up, down = up_ref[...].astype(F32), down_ref[...].astype(F32)
    near = keep_ref[...] + up[:size] + down[:size]
    two = up_two_ref[...].astype(F32) + down_two_ref[...].astype(F32)
    return near + (two + far_ref[...].astype(F32))


def residual_kernel(rows_ref, *refs):
    *addends, out_ref = refs
    out_ref[...] = (rows_ref[...].astype(F32) + total(*addends)).astype(BF16)


def norm_backward(step, order, stash, *arrays):
    in_vmem = pl.BlockSpec(memory_space=pltpu.VMEM)
    return call(
        functools.partial(norm_backward_kernel, step),
        shaped(stash.shape[1:], BF16),
        in_specs=[pl.BlockSpec(memory_space=pltpu.SMEM)] + [in_vmem] * (1 + len(arrays)),
    )(order, stash, *arrays)


def norm_backward_kernel(step, order_ref, stash_ref, grad_ref, gain_ref, *refs):
    *addends, out_ref = refs
    rows = stash_ref[order_ref[0, step]]
    _, scaled, inv_scale = normalize(rows.astype(F32), gain_ref[...])
    d_scaled = total(*addends) * gain_ref[...]
    d_rows = inv_scale * (
        d_scaled
        - jnp.mean(d_scaled, axis=-1, keepdims=True)
        - scaled * jnp.mean(d_scaled * scaled, axis=-1, keepdims=True)
    )
    out_ref[...] = (grad_ref[...].astype(F32) + d_rows).astype(BF16)


def gathered(piece_refs):
    if all(ref.shape[0] % 16 == 0 for ref in piece_refs):
        return jnp.concatenate([ref[...] for ref in piece_refs], axis=0)
    return jnp.concatenate([ref[...].astype(F32) for ref in piece_refs], axis=0).astype(BF16)


def dot(a, b, dims=(((1,), (0,)), ((), ()))):
    return lax.dot_general(a, b, dims, preferred_element_type=F32)


def probabilities(query, key, visible):
    scores = dot(query, key, TRANSPOSED) * (1.0 / math.sqrt(HD))
    scores = jnp.where(visible, scores, -jnp.inf)
    shifted = jnp.exp(scores - jnp.max(scores, axis=-1, keepdims=True))
    return shifted / jnp.sum(shifted, axis=-1, keepdims=True)


def head_slices(qkv, head):
    inner = qkv.shape[1] // 3
    return [qkv[:, j * inner + head * HD : j * inner + (head + 1) * HD] for j in range(3)]


def add_projections(sums, rows, weight_refs):
    inner = weight_refs[0].shape[0]
    for j, weight_ref in enumerate(weight_refs):
        sums[:, j * inner : (j + 1) * inner] += dot(rows, weight_ref[...], TRANSPOSED)


def forward_kernel(steps_in, pieces, *refs):
    piece_refs, (place_ref, *refs) = refs[:pieces], refs[pieces:]
    *weight_refs, proj_ref, visible_ref, own_ref, other_ref, sums, mixed_ref = refs
    step = pl.program_id(0)
    inner = mixed_ref.shape[1]

    @pl.when(step == 0)
    def _():
        sums[...] = jnp.zeros_like(sums)

    @pl.when(step < steps_in)
    def _():
        add_projections(sums, gathered(piece_refs), weight_refs)

    @pl.when(step == steps_in - 1)
    def _():
        qkv = dot(place_ref[...], sums[...].astype(BF16)).astype(BF16)
        visible = visible_ref[...] > 0.0
        for head in range(mixed_ref.shape[1] // HD):
            query, key, value = head_slices(qkv, head)
            probs = probabilities(query, key, visible).astype(BF16)
            mixed_ref[:, head * HD : (head + 1) * HD] = dot(probs, value).astype(BF16)

    @pl.when(step >= steps_in)
    def _():
        rows = dot(mixed_ref[...], proj_ref[...])
        half = rows.shape[0] // 2
        own_ref[...] = rows[:half].astype(BF16)
        other_ref[...] = rows[half:].astype(BF16)


def section_call(kernel, pieces, weights, proj, visible, extra, steps, forward):
    tokens, (inner, width) = visible.shape[0], proj.shape
    steps_in, steps_out = steps
    block_in, block_out = width // steps_in, width // steps_out
    first = lambda i: (0, jnp.minimum(i, steps_in - 1))
    second = lambda i: (0, jnp.maximum(i - steps_in, 0))
    whole = lambda i: (0, 0)
    arrays, place = pieces
    inputs = [*arrays, place]
    in_specs = [pl.BlockSpec((piece.shape[0], block_in), first) for piece in arrays]
    in_specs.append(pl.BlockSpec(place.shape, whole))
    weight_spec = (block_in, first) if forward else (block_out, second)
    proj_spec = (block_out, second) if forward else (block_in, first)
    in_specs += [pl.BlockSpec((w.shape[0], weight_spec[0]), weight_spec[1]) for w in weights]
    in_specs += [pl.BlockSpec((inner, proj_spec[0]), proj_spec[1])]
    inputs += [*weights, proj, visible, *extra]
    in_specs += [pl.BlockSpec(array.shape, whole) for array in (visible, *extra)]
    scratch = [(3 * inner, F32), (inner, BF16)] if forward else [(inner, F32), (3 * inner, BF16)]
    return call(
        functools.partial(kernel, steps_in, len(arrays)),
        [shaped((tokens // 2, width), BF16)] * 2,
        flops=8 * tokens * inner * width,
        moved=24 * inner * width + 8 * tokens * width,
        grid=(steps_in + steps_out,),
        in_specs=in_specs,
        out_specs=[pl.BlockSpec((tokens // 2, block_out), second)] * 2,
        scratch_shapes=[pltpu.VMEM((tokens, columns), dtype) for columns, dtype in scratch],
    )(*inputs)


def forward_section(pieces, weights, proj, visible):
    return section_call(
        forward_kernel, pieces, weights, proj, visible, (), (6, 4), True
    )


def qkv_kernel(rows_ref, place_ref, *refs):
    *weight_refs, out_ref, sums = refs
    step = pl.program_id(0)

    @pl.when(step == 0)
    def _():
        sums[...] = jnp.zeros_like(sums)

    add_projections(sums, rows_ref[...], weight_refs)

    @pl.when(step == pl.num_programs(0) - 1)
    def _():
        out_ref[...] = dot(place_ref[...], sums[...].astype(BF16)).astype(BF16)


def qkv_section(rows, place, weights):
    tokens, width = rows.shape
    columns = sum(w.shape[0] for w in weights)
    blocks = 6
    block = width // blocks
    column = lambda i: (0, i)
    whole = lambda i: (0, 0)
    return call(
        qkv_kernel,
        shaped((tokens, columns), BF16),
        flops=2 * tokens * columns * width,
        moved=4 * columns * width,
        grid=(blocks,),
        in_specs=[pl.BlockSpec((tokens, block), column), pl.BlockSpec(place.shape, whole)]
        + [pl.BlockSpec((w.shape[0], block), column) for w in weights],
        out_specs=pl.BlockSpec((tokens, columns), whole),
        scratch_shapes=[pltpu.VMEM((tokens, columns), F32)],
    )(rows, place, *weights)


def backward_kernel(steps_in, pieces, *refs):
    piece_refs, (place_ref, *refs) = refs[:pieces], refs[pieces:]
    *weight_refs, proj_ref, visible_ref, qkv_ref, own_ref, other_ref, sums, d_qkv_ref = refs
    step = pl.program_id(0)

    @pl.when(step == 0)
    def _():
        sums[...] = jnp.zeros_like(sums)

    @pl.when(step < steps_in)
    def _():
        sums[...] += dot(gathered(piece_refs), proj_ref[...], TRANSPOSED)

    @pl.when(step == steps_in - 1)
    def _():
        d_mixed = dot(place_ref[...], sums[...].astype(BF16)).astype(BF16)
        inner = d_mixed.shape[1]
        visible = visible_ref[...] > 0.0
        qkv = qkv_ref[...]
        for head in range(inner // HD):
            query, key, value = head_slices(qkv, head)
            mixed = d_mixed[:, head * HD : (head + 1) * HD]
            probs = probabilities(query, key, visible)
            d_probs = dot(mixed, value, TRANSPOSED)
            probs_turned = probs.T.astype(BF16)
            d_scores = (
                probs
                * (d_probs - jnp.sum(d_probs * probs, axis=-1, keepdims=True))
                * (1.0 / math.sqrt(HD))
            )
            parts = (
                dot(d_scores.astype(BF16), key),
                dot(d_scores.T.astype(BF16), query),
                dot(probs_turned, mixed),
            )
            for j, part in enumerate(parts):
                place = j * inner + head * HD
                d_qkv_ref[:, place : place + HD] = part.astype(BF16)

    @pl.when(step >= steps_in)
    def _():
        inner = weight_refs[0].shape[0]
        rows = sum(
            dot(d_qkv_ref[:, j * inner : (j + 1) * inner], weight_ref[...])
            for j, weight_ref in enumerate(weight_refs)
        )
        half = rows.shape[0] // 2
        own_ref[...] = rows[:half].astype(BF16)
        other_ref[...] = rows[half:].astype(BF16)


def backward_section(pieces, weights, proj, visible, qkv):
    return section_call(
        backward_kernel, pieces, weights, proj, visible, (qkv,), (4, 6), False
    )


def on_device(
    new_inputs,
    new_grads,
    forward_state,
    backward_state,
    stashed,
    new_docs,
    state_docs,
    stash_docs,
    stash_order,
    norm_gain,
    qkv_weight,
    out_weight,
):
    proj = out_weight[0]
    pipe_index = lax.axis_index("pipe")
    last_pipe = lax.axis_size("pipe") - 1
    size = forward_state.shape[1]
    tokens = size * YS * ZS
    y_index, z_index = lax.axis_index("y"), lax.axis_index("z")

    def tokens_of(blocks):
        starts = [((y_index + y) % YS * ZS + (z_index + z + ZS) % ZS) * size for y, z in blocks]
        return jnp.concatenate([start + lax.iota(jnp.int32, size) for start in starts])

    positions = tokens_of([(y, z) for y in range(YS) for z in Z_ORDER])

    def place_of(order):
        return (positions[:, None] == order[None, :]).astype(BF16)

    ring_place = place_of(tokens_of([(y, z) for y in range(YS) for z in EARLY + LATE]))
    pairs_place = place_of(tokens_of([(y, z) for z in Z_ORDER for y in range(YS)]))
    by_z = [z - z_index for z in range(ZS)]
    stash_place = place_of(tokens_of([(y, z) for z in by_z for y in range(YS)]))
    halves_place = place_of(tokens_of([(y, z) for y in range(YS) for z in by_z]))
    chosen = positions[:, None] == lax.iota(jnp.int32, tokens)[None, :]
    before = positions[:, None] >= positions[None, :]

    def visible_from(ids):
        ids = jnp.sum(jnp.where(chosen, ids[None, :], 0), axis=1)
        return jnp.where(before & (ids[:, None] == ids[None, :]), 1.0, 0.0).astype(F32)

    stash, stored_visible = stashed[0], []
    for phase in range(STEPS):
        ids = lax.dynamic_index_in_dim(stash_docs[0], stash_order[0, phase], 0, keepdims=False)
        stored_visible.append(visible_from(ids))
    visible = [visible_from(state_docs[0]), None]

    rows, grads = forward_state[0], backward_state[0]
    normed = call(start_kernel, shaped(rows.shape, BF16))(rows, norm_gain)
    stash_swapped = y_swap(after(stash, normed))
    stash_pieces = []

    def stash_ready(arrived):
        other = after(stash_swapped, arrived)
        stash_pieces.extend(stash_rows(stash_order, stash, other, norm_gain))
        return stash_pieces[0]

    arrays = gather_z_first(normed, stash_ready)
    stash_pieces = [lax.all_gather(piece, "z", axis=0, tiled=True) for piece in stash_pieces]
    grads_own = exchange(stack_rows(*[after(grads, *arrays[:ZS])] * ZS))
    grad_pieces = ([grads_own, y_swap(grads_own)], halves_place)
    weight = jnp.transpose(after(qkv_weight, *arrays[:ZS])[0], (1, 2, 0))
    weights = [weight.reshape(-1, weight.shape[2])]
    pieces = ([after(arrays[0], grads_own)] + arrays[1:], ring_place)

    qkv_stash = [None, None]
    for phase in range(STEPS):
        own, other = forward_section(pieces, weights, proj, visible[phase])
        got = y_swap(other)
        if phase == 0:
            qkv_stash[0] = qkv_section(after(stash_pieces[0], own), stash_place, weights)
            ids = from_behind(after(state_docs[0], own), 1)
            visible[1] = visible_from(jnp.where(pipe_index == 0, new_docs[0], ids))
            entering = (new_inputs[0], y_swap(after(new_inputs[0], own)))
        arrays, grad_place = grad_pieces
        grad_pieces = ([after(arrays[0], own)] + arrays[1:], grad_place)
        d_own, d_other = backward_section(
            grad_pieces, weights, proj, stored_visible[phase], qkv_stash[phase]
        )
        sums = scatter_sum(own, after(got, d_own))
        d_got = y_swap(d_other)
        if phase == 0:
            qkv_stash[1] = qkv_section(after(stash_pieces[1], d_own), stash_place, weights)
            d_got = after(d_got, qkv_stash[1])
        d_sums = scatter_sum(d_own, d_got)
        rows_next = call(residual_kernel, shaped(rows.shape, BF16))(rows, *sums)
        grads_next = norm_backward(phase, stash_order, stash, grads, norm_gain, *d_sums)
        if phase + 1 < STEPS:
            at_end, at_start = pipe_index == last_pipe, pipe_index == 0
            came = (from_behind(rows_next, 1), from_behind_swapped(rows_next, 1))
            came = [jnp.where(at_start, new, old) for new, old in zip(entering, came)]
            rows = came[0]
            pieces = (gather_y_first(normalize_rows(*came, norm_gain)), pairs_place)
            grads = jnp.where(at_end, new_grads[0], from_behind(grads_next, -1))
            grad_pieces = (gather_z_first(grads), ring_place)
    return (rows_next[None], grads_next[None])


def solution(mesh):
    split = Mesh(mesh.devices.reshape(-1, YS, ZS), ("pipe", "y", "z"))
    tensor = ("y", "z")
    return jax.shard_map(
        on_device,
        mesh=split,
        in_specs=(
            P(None, tensor, None),
            P(None, tensor, None),
            P("pipe", tensor, None),
            P("pipe", tensor, None),
            P("pipe", None, tensor, None),
            P(),
            P("pipe", None),
            P("pipe", None, None),
            P("pipe", None),
            P("pipe", None),
            P("pipe", None, None, tensor),
            P("pipe", tensor, None),
        ),
        out_specs=(P("pipe", tensor, None), P("pipe", tensor, None)),
        check_vma=False,
    )
```

```python
import functools
import math

import jax
import jax.numpy as jnp
from jax import lax
from jax.experimental import pallas as pl
from jax.experimental.pallas import tpu as pltpu
from jax.sharding import Mesh
from jax.sharding import PartitionSpec as P

HD = 128
STEPS = 2
NORM_EPS = 1e-05
TRANSPOSED = (((1,), (1,)), ((), ()))
YS, ZS = 2, 8
Z_ORDER = (0, 1, -3, -1, 3, 2, -2, 4)
EARLY, LATE = (0, 1, -1, 2, -2), (-3, 3, 4)
BF16, F32 = jnp.bfloat16, jnp.float32
VMEM_LIMIT = 48 * 1024 * 1024


def from_behind(value, steps):
    count = lax.axis_size("pipe")
    first, last = (max(0, -steps), min(count, count - steps))
    return lax.ppermute(value, "pipe", [(source, source + steps) for source in range(first, last)])


def from_behind_swapped(value, steps):
    count = lax.axis_size("pipe")
    first, last = (max(0, -steps), min(count, count - steps))
    pairs = [
        (s * YS + y, (s + steps) * YS + 1 - y) for s in range(first, last) for y in range(YS)
    ]
    return lax.ppermute(value, ("pipe", "y"), pairs)


def y_swap(value):
    return lax.ppermute(value, "y", [(0, 1), (1, 0)])


def after(value, *others):
    return lax.optimization_barrier((value, *others))[0]


def z_shift(value, steps):
    return lax.ppermute(value, "z", [(z, (z + steps) % ZS) for z in range(ZS)])


def ring(piece, between=None):
    held = {0: piece}
    ahead = behind = piece
    for hop in range(1, 5):
        if hop == 2 and between is not None:
            ready = between(ahead)
            ahead, behind = after(ahead, ready), after(behind, ready)
        ahead = z_shift(ahead, 1)
        held[-hop if hop < 4 else 4] = ahead
        if hop < 4:
            behind = z_shift(behind, -1)
            held[hop] = behind
    return held


def gather_z_first(piece, between=None):
    held = ring(piece, between)
    parts = [y_swap(stack_rows(*[held[z] for z in group])) for group in (EARLY, LATE)]
    return [held[z] for z in EARLY + LATE] + parts


def gather_y_first(piece):
    held = ring(piece)
    return [held[z] for z in Z_ORDER]


def call(kernel, out_shape, flops=0, moved=0, **options):
    if flops:
        options["cost_estimate"] = pl.CostEstimate(
            flops=flops, bytes_accessed=moved, transcendentals=0
        )
    return pl.pallas_call(
        kernel,
        out_shape=out_shape,
        compiler_params=pltpu.CompilerParams(vmem_limit_bytes=VMEM_LIMIT),
        **options,
    )


def shaped(shape, dtype):
    return jax.ShapeDtypeStruct(shape, dtype)


def normalize(values, gain):
    centered = values - jnp.mean(values, axis=-1, keepdims=True)
    inv_scale = lax.rsqrt(jnp.mean(centered * centered, axis=-1, keepdims=True) + NORM_EPS)
    scaled = centered * inv_scale
    return (scaled * gain, scaled, inv_scale)


def normalized(ref, gain_ref):
    return normalize(ref[...].astype(F32), gain_ref[...])[0]


def normalize_kernel(a_ref, b_ref, gain_ref, out_ref):
    rows = [normalized(a_ref, gain_ref), normalized(b_ref, gain_ref)]
    out_ref[...] = jnp.concatenate(rows, axis=0).astype(BF16)


def normalize_rows(a, b, gain):
    shape = shaped((2 * a.shape[0], a.shape[1]), BF16)
    return call(normalize_kernel, shape)(a, b, gain)


def start_kernel(rows_ref, grads_ref, gain_ref, out_ref):
    rows = [normalized(rows_ref, gain_ref), grads_ref[...].astype(F32)]
    out_ref[...] = jnp.concatenate(rows, axis=0).astype(BF16)


def stash_kernel(order_ref, own_ref, other_ref, gain_ref, *out_refs):
    for step, out_ref in enumerate(out_refs):
        slot = order_ref[0, step]
        rows = [normalized(ref.at[slot], gain_ref) for ref in (own_ref, other_ref)]
        out_ref[...] = jnp.concatenate(rows, axis=0).astype(BF16)


def stash_rows(order, own, other, gain):
    steps, size, width = own.shape
    in_vmem = pl.BlockSpec(memory_space=pltpu.VMEM)
    return call(
        stash_kernel,
        [shaped((YS * size, width), BF16)] * steps,
        in_specs=[pl.BlockSpec(memory_space=pltpu.SMEM)] + [in_vmem] * 3,
    )(order, own, other, gain)


def stack_kernel(*refs):
    *piece_refs, out_ref = refs
    rows = [ref[...].astype(F32) for ref in piece_refs]
    out_ref[...] = jnp.concatenate(rows, axis=0).astype(BF16)


def stack_rows(*pieces):
    tokens = sum(piece.shape[0] for piece in pieces)
    return call(stack_kernel, shaped((tokens, pieces[0].shape[1]), BF16))(*pieces)


def split_kernel(size, own_ref, got_ref, keep_ref, up_ref, down_ref, up_two_ref, down_two_ref, far_ref):
    rows = own_ref[...].astype(F32) + got_ref[...].astype(F32)
    keep_ref[...] = rows[:size]
    up_ref[...] = rows[size : 3 * size].astype(BF16)
    down_ref[...] = rows[3 * size : 5 * size].astype(BF16)
    up_two_ref[...] = rows[5 * size : 6 * size].astype(BF16)
    down_two_ref[...] = rows[6 * size : 7 * size].astype(BF16)
    far_ref[...] = rows[7 * size :]


def far_kernel(size, far_ref, up_ref, down_ref, out_ref):
    up, down = up_ref[...].astype(F32), down_ref[...].astype(F32)
    out_ref[...] = (far_ref[...] + up[size:] + down[size:]).astype(BF16)


def scatter_sum(own, got):
    half, width = own.shape
    size, block = half // ZS, width // 3
    outs = [(size, F32), (2 * size, BF16), (2 * size, BF16), (size, BF16), (size, BF16), (size, F32)]
    column = lambda tokens: pl.BlockSpec((tokens, block), lambda i: (0, i))
    keep, up, down, up_two, down_two, far = call(
        functools.partial(split_kernel, size),
        [shaped((tokens, width), dtype) for tokens, dtype in outs],
        grid=(width // block,),
        in_specs=[column(half), column(half)],
        out_specs=[column(tokens) for tokens, _ in outs],
    )(own, got)
    up, down = z_shift(up, 1), z_shift(down, -1)
    up_two, down_two = z_shift(up_two, 2), z_shift(down_two, -2)
    far = call(functools.partial(far_kernel, size), shaped((size, width), BF16))(far, up, down)
    return (keep, up, down, up_two, down_two, z_shift(far, 4))


def total(keep_ref, up_ref, down_ref, up_two_ref, down_two_ref, far_ref):
    size = keep_ref.shape[0]
    up, down = up_ref[...].astype(F32), down_ref[...].astype(F32)
    near = keep_ref[...] + up[:size] + down[:size]
    two = up_two_ref[...].astype(F32) + down_two_ref[...].astype(F32)
    return near + (two + far_ref[...].astype(F32))


def residual_kernel(rows_ref, *refs):
    *addends, out_ref = refs
    out_ref[...] = (rows_ref[...].astype(F32) + total(*addends)).astype(BF16)


def norm_backward(step, order, stash, *arrays):
    in_vmem = pl.BlockSpec(memory_space=pltpu.VMEM)
    return call(
        functools.partial(norm_backward_kernel, step),
        shaped(stash.shape[1:], BF16),
        in_specs=[pl.BlockSpec(memory_space=pltpu.SMEM)] + [in_vmem] * (1 + len(arrays)),
    )(order, stash, *arrays)


def norm_backward_kernel(step, order_ref, stash_ref, grad_ref, gain_ref, *refs):
    *addends, out_ref = refs
    rows = stash_ref[order_ref[0, step]]
    _, scaled, inv_scale = normalize(rows.astype(F32), gain_ref[...])
    d_scaled = total(*addends) * gain_ref[...]
    d_rows = inv_scale * (
        d_scaled
        - jnp.mean(d_scaled, axis=-1, keepdims=True)
        - scaled * jnp.mean(d_scaled * scaled, axis=-1, keepdims=True)
    )
    out_ref[...] = (grad_ref[...].astype(F32) + d_rows).astype(BF16)


def gathered(piece_refs, part, size):
    if part is None:
        return jnp.concatenate([ref[...] for ref in piece_refs], axis=0)
    pieces = [ref[...].astype(F32) for ref in piece_refs]
    span = pieces[0].shape[0]
    blocks = [
        piece[start + part * size : start + (part + 1) * size]
        for piece in pieces
        for start in range(0, piece.shape[0], span)
    ]
    return jnp.concatenate(blocks, axis=0).astype(BF16)


def dot(a, b, dims=(((1,), (0,)), ((), ()))):
    return lax.dot_general(a, b, dims, preferred_element_type=F32)


def probabilities(query, key, visible):
    scores = dot(query, key, TRANSPOSED) * (1.0 / math.sqrt(HD))
    scores = jnp.where(visible, scores, -jnp.inf)
    shifted = jnp.exp(scores - jnp.max(scores, axis=-1, keepdims=True))
    return shifted / jnp.sum(shifted, axis=-1, keepdims=True)


def head_slices(qkv, head):
    inner = qkv.shape[1] // 3
    return [qkv[:, j * inner + head * HD : j * inner + (head + 1) * HD] for j in range(3)]


def add_projections(sums, rows, weight_refs):
    inner = weight_refs[0].shape[0]
    for j, weight_ref in enumerate(weight_refs):
        sums[:, j * inner : (j + 1) * inner] += dot(rows, weight_ref[...], TRANSPOSED)


def forward_kernel(steps_in, pieces, part, *refs):
    piece_refs, (place_ref, *refs) = refs[:pieces], refs[pieces:]
    *weight_refs, proj_ref, visible_ref, own_ref, other_ref, sums, mixed_ref = refs
    step = pl.program_id(0)
    inner = mixed_ref.shape[1]

    @pl.when(step == 0)
    def _():
        sums[...] = jnp.zeros_like(sums)

    @pl.when(step < steps_in)
    def _():
        add_projections(sums, gathered(piece_refs, part, visible_ref.shape[0] // (YS * ZS)), weight_refs)

    @pl.when(step == steps_in - 1)
    def _():
        qkv = dot(place_ref[...], sums[...].astype(BF16)).astype(BF16)
        visible = visible_ref[...] > 0.0
        for head in range(mixed_ref.shape[1] // HD):
            query, key, value = head_slices(qkv, head)
            probs = probabilities(query, key, visible).astype(BF16)
            mixed_ref[:, head * HD : (head + 1) * HD] = dot(probs, value).astype(BF16)

    @pl.when(step >= steps_in)
    def _():
        rows = dot(mixed_ref[...], proj_ref[...])
        half = rows.shape[0] // 2
        own_ref[...] = rows[:half].astype(BF16)
        other_ref[...] = rows[half:].astype(BF16)


def section_call(kernel, pieces, weights, proj, visible, extra, steps, forward):
    tokens, (inner, width) = visible.shape[0], proj.shape
    steps_in, steps_out = steps
    block_in, block_out = width // steps_in, width // steps_out
    first = lambda i: (0, jnp.minimum(i, steps_in - 1))
    second = lambda i: (0, jnp.maximum(i - steps_in, 0))
    whole = lambda i: (0, 0)
    arrays, part, place = pieces
    inputs = [*arrays, place]
    in_specs = [pl.BlockSpec((piece.shape[0], block_in), first) for piece in arrays]
    in_specs.append(pl.BlockSpec(place.shape, whole))
    weight_spec = (block_in, first) if forward else (block_out, second)
    proj_spec = (block_out, second) if forward else (block_in, first)
    in_specs += [pl.BlockSpec((w.shape[0], weight_spec[0]), weight_spec[1]) for w in weights]
    in_specs += [pl.BlockSpec((inner, proj_spec[0]), proj_spec[1])]
    inputs += [*weights, proj, visible, *extra]
    in_specs += [pl.BlockSpec(array.shape, whole) for array in (visible, *extra)]
    scratch = [(3 * inner, F32), (inner, BF16)] if forward else [(inner, F32), (3 * inner, BF16)]
    return call(
        functools.partial(kernel, steps_in, len(arrays), part),
        [shaped((tokens // 2, width), BF16)] * 2,
        flops=8 * tokens * inner * width,
        moved=24 * inner * width + 8 * tokens * width,
        grid=(steps_in + steps_out,),
        in_specs=in_specs,
        out_specs=[pl.BlockSpec((tokens // 2, block_out), second)] * 2,
        scratch_shapes=[pltpu.VMEM((tokens, columns), dtype) for columns, dtype in scratch],
    )(*inputs)


def forward_section(pieces, weights, proj, visible):
    return section_call(
        forward_kernel, pieces, weights, proj, visible, (), (6, 4), True
    )


def qkv_kernel(rows_ref, place_ref, *refs):
    *weight_refs, out_ref, sums = refs
    step = pl.program_id(0)

    @pl.when(step == 0)
    def _():
        sums[...] = jnp.zeros_like(sums)

    add_projections(sums, rows_ref[...], weight_refs)

    @pl.when(step == pl.num_programs(0) - 1)
    def _():
        out_ref[...] = dot(place_ref[...], sums[...].astype(BF16)).astype(BF16)


def qkv_section(rows, place, weights):
    tokens, width = rows.shape
    columns = sum(w.shape[0] for w in weights)
    blocks = 6
    block = width // blocks
    column = lambda i: (0, i)
    whole = lambda i: (0, 0)
    return call(
        qkv_kernel,
        shaped((tokens, columns), BF16),
        flops=2 * tokens * columns * width,
        moved=4 * columns * width,
        grid=(blocks,),
        in_specs=[pl.BlockSpec((tokens, block), column), pl.BlockSpec(place.shape, whole)]
        + [pl.BlockSpec((w.shape[0], block), column) for w in weights],
        out_specs=pl.BlockSpec((tokens, columns), whole),
        scratch_shapes=[pltpu.VMEM((tokens, columns), F32)],
    )(rows, place, *weights)


def backward_kernel(steps_in, pieces, part, *refs):
    piece_refs, (place_ref, *refs) = refs[:pieces], refs[pieces:]
    *weight_refs, proj_ref, visible_ref, qkv_ref, own_ref, other_ref, sums, d_qkv_ref = refs
    step = pl.program_id(0)

    @pl.when(step == 0)
    def _():
        sums[...] = jnp.zeros_like(sums)

    @pl.when(step < steps_in)
    def _():
        sums[...] += dot(gathered(piece_refs, part, visible_ref.shape[0] // (YS * ZS)), proj_ref[...], TRANSPOSED)

    @pl.when(step == steps_in - 1)
    def _():
        d_mixed = dot(place_ref[...], sums[...].astype(BF16)).astype(BF16)
        inner = d_mixed.shape[1]
        visible = visible_ref[...] > 0.0
        qkv = qkv_ref[...]
        for head in range(inner // HD):
            query, key, value = head_slices(qkv, head)
            mixed = d_mixed[:, head * HD : (head + 1) * HD]
            probs = probabilities(query, key, visible)
            d_probs = dot(mixed, value, TRANSPOSED)
            probs_turned = probs.T.astype(BF16)
            d_scores = (
                probs
                * (d_probs - jnp.sum(d_probs * probs, axis=-1, keepdims=True))
                * (1.0 / math.sqrt(HD))
            )
            parts = (
                dot(d_scores.astype(BF16), key),
                dot(d_scores.T.astype(BF16), query),
                dot(probs_turned, mixed),
            )
            for j, part in enumerate(parts):
                place = j * inner + head * HD
                d_qkv_ref[:, place : place + HD] = part.astype(BF16)

    @pl.when(step >= steps_in)
    def _():
        inner = weight_refs[0].shape[0]
        rows = sum(
            dot(d_qkv_ref[:, j * inner : (j + 1) * inner], weight_ref[...])
            for j, weight_ref in enumerate(weight_refs)
        )
        half = rows.shape[0] // 2
        own_ref[...] = rows[:half].astype(BF16)
        other_ref[...] = rows[half:].astype(BF16)


def backward_section(pieces, weights, proj, visible, qkv):
    return section_call(
        backward_kernel, pieces, weights, proj, visible, (qkv,), (4, 6), False
    )


def on_device(
    new_inputs,
    new_grads,
    forward_state,
    backward_state,
    stashed,
    new_docs,
    state_docs,
    stash_docs,
    stash_order,
    norm_gain,
    qkv_weight,
    out_weight,
):
    proj = out_weight[0]
    pipe_index = lax.axis_index("pipe")
    last_pipe = lax.axis_size("pipe") - 1
    size = forward_state.shape[1]
    tokens = size * YS * ZS
    y_index, z_index = lax.axis_index("y"), lax.axis_index("z")

    def tokens_of(blocks):
        starts = [((y_index + y) % YS * ZS + (z_index + z + ZS) % ZS) * size for y, z in blocks]
        return jnp.concatenate([start + lax.iota(jnp.int32, size) for start in starts])

    positions = tokens_of([(y, z) for y in range(YS) for z in Z_ORDER])

    def place_of(order):
        return (positions[:, None] == order[None, :]).astype(BF16)

    ring_place = place_of(tokens_of([(y, z) for y in range(YS) for z in EARLY + LATE]))
    pairs_place = place_of(tokens_of([(y, z) for z in Z_ORDER for y in range(YS)]))
    by_z = [z - z_index for z in range(ZS)]
    stash_place = place_of(tokens_of([(y, z) for z in by_z for y in range(YS)]))
    chosen = positions[:, None] == lax.iota(jnp.int32, tokens)[None, :]
    before = positions[:, None] >= positions[None, :]

    def visible_from(ids):
        ids = jnp.sum(jnp.where(chosen, ids[None, :], 0), axis=1)
        return jnp.where(before & (ids[:, None] == ids[None, :]), 1.0, 0.0).astype(F32)

    stash, stored_visible = stashed[0], []
    for phase in range(STEPS):
        ids = lax.dynamic_index_in_dim(stash_docs[0], stash_order[0, phase], 0, keepdims=False)
        stored_visible.append(visible_from(ids))
    visible = [visible_from(state_docs[0]), None]

    rows, grads = forward_state[0], backward_state[0]
    size, width = rows.shape
    start = call(start_kernel, shaped((2 * size, width), BF16))(rows, grads, norm_gain)
    stash_swapped = y_swap(after(stash, start))
    stash_pieces = []

    def stash_ready(arrived):
        other = after(stash_swapped, arrived)
        stash_pieces.extend(stash_rows(stash_order, stash, other, norm_gain))
        return stash_pieces[0]

    arrays = gather_z_first(start, stash_ready)
    stash_pieces = [lax.all_gather(piece, "z", axis=0, tiled=True) for piece in stash_pieces]
    weight = jnp.transpose(after(qkv_weight, *arrays[:ZS])[0], (1, 2, 0))
    weights = [weight.reshape(-1, weight.shape[2])]
    pieces, grad_pieces = (arrays, 0, ring_place), (arrays, 1, ring_place)

    qkv_stash = [None, None]
    for phase in range(STEPS):
        own, other = forward_section(pieces, weights, proj, visible[phase])
        got = y_swap(other)
        if phase == 0:
            qkv_stash[0] = qkv_section(after(stash_pieces[0], own), stash_place, weights)
            ids = from_behind(after(state_docs[0], own), 1)
            visible[1] = visible_from(jnp.where(pipe_index == 0, new_docs[0], ids))
            entering = (new_inputs[0], y_swap(after(new_inputs[0], own)))
        arrays, part, place = grad_pieces
        grad_pieces = ([after(arrays[0], own)] + arrays[1:], part, place)
        d_own, d_other = backward_section(
            grad_pieces, weights, proj, stored_visible[phase], qkv_stash[phase]
        )
        sums = scatter_sum(own, after(got, d_own))
        d_got = y_swap(d_other)
        if phase == 0:
            qkv_stash[1] = qkv_section(after(stash_pieces[1], d_own), stash_place, weights)
            d_got = after(d_got, qkv_stash[1])
        if phase == 0:
            sums = (after(sums[0], d_got), *sums[1:])
        d_sums = scatter_sum(d_own, d_got)
        rows_next = call(residual_kernel, shaped(rows.shape, BF16))(rows, *sums)
        grads_next = norm_backward(phase, stash_order, stash, grads, norm_gain, *d_sums)
        if phase + 1 < STEPS:
            at_end, at_start = pipe_index == last_pipe, pipe_index == 0
            came = (from_behind(rows_next, 1), from_behind_swapped(rows_next, 1))
            came = [jnp.where(at_start, new, old) for new, old in zip(entering, came)]
            rows = came[0]
            arrays = gather_y_first(normalize_rows(*came, norm_gain))
            grads = jnp.where(at_end, new_grads[0], from_behind(grads_next, -1))
            grad_pieces = (gather_z_first(grads), 0, ring_place)
            pieces = (arrays, None, pairs_place)
    return (rows_next[None], grads_next[None])


def solution(mesh):
    split = Mesh(mesh.devices.reshape(-1, YS, ZS), ("pipe", "y", "z"))
    tensor = ("y", "z")
    return jax.shard_map(
        on_device,
        mesh=split,
        in_specs=(
            P(None, tensor, None),
            P(None, tensor, None),
            P("pipe", tensor, None),
            P("pipe", tensor, None),
            P("pipe", None, tensor, None),
            P(),
            P("pipe", None),
            P("pipe", None, None),
            P("pipe", None),
            P("pipe", None),
            P("pipe", None, None, tensor),
            P("pipe", tensor, None),
        ),
        out_specs=(P("pipe", tensor, None), P("pipe", tensor, None)),
        check_vma=False,
    )
```

```python
import functools
import math

import jax
import jax.numpy as jnp
from jax import lax
from jax.experimental import pallas as pl
from jax.experimental.pallas import tpu as pltpu
from jax.sharding import Mesh
from jax.sharding import PartitionSpec as P

HD = 128
STEPS = 2
NORM_EPS = 1e-05
TRANSPOSED = (((1,), (1,)), ((), ()))
YS, ZS = 2, 8
Z_ORDER = (0, 1, -3, -1, 3, 2, -2, 4)
EARLY, LATE = (0, 1, -1, 2, -2), (-3, 3, 4)
BF16, F32 = jnp.bfloat16, jnp.float32
VMEM_LIMIT = 48 * 1024 * 1024


def from_behind(value, steps):
    count = lax.axis_size("pipe")
    first, last = (max(0, -steps), min(count, count - steps))
    return lax.ppermute(value, "pipe", [(source, source + steps) for source in range(first, last)])


def from_behind_swapped(value, steps):
    count = lax.axis_size("pipe")
    first, last = (max(0, -steps), min(count, count - steps))
    pairs = [
        (s * YS + y, (s + steps) * YS + 1 - y) for s in range(first, last) for y in range(YS)
    ]
    return lax.ppermute(value, ("pipe", "y"), pairs)


def y_swap(value):
    return lax.ppermute(value, "y", [(0, 1), (1, 0)])


def after(value, *others):
    return lax.optimization_barrier((value, *others))[0]


def z_shift(value, steps):
    return lax.ppermute(value, "z", [(z, (z + steps) % ZS) for z in range(ZS)])


def ring(piece, between=None):
    held = {0: piece}
    ahead = behind = piece
    for hop in range(1, 5):
        if hop == 2 and between is not None:
            ready = between(ahead)
            ahead, behind = after(ahead, ready), after(behind, ready)
        ahead = z_shift(ahead, 1)
        held[-hop if hop < 4 else 4] = ahead
        if hop < 4:
            behind = z_shift(behind, -1)
            held[hop] = behind
    return held


def gather_z_first(piece, between=None):
    held = ring(piece, between)
    parts = [y_swap(stack_rows(*[held[z] for z in group])) for group in (EARLY, LATE)]
    return [held[z] for z in EARLY + LATE] + parts


def gather_y_first(piece):
    held = ring(piece)
    return [held[z] for z in Z_ORDER]


def call(kernel, out_shape, flops=0, moved=0, **options):
    if flops:
        options["cost_estimate"] = pl.CostEstimate(
            flops=flops, bytes_accessed=moved, transcendentals=0
        )
    return pl.pallas_call(
        kernel,
        out_shape=out_shape,
        compiler_params=pltpu.CompilerParams(vmem_limit_bytes=VMEM_LIMIT),
        **options,
    )


def shaped(shape, dtype):
    return jax.ShapeDtypeStruct(shape, dtype)


def normalize(values, gain):
    centered = values - jnp.mean(values, axis=-1, keepdims=True)
    inv_scale = lax.rsqrt(jnp.mean(centered * centered, axis=-1, keepdims=True) + NORM_EPS)
    scaled = centered * inv_scale
    return (scaled * gain, scaled, inv_scale)


def normalized(ref, gain_ref):
    return normalize(ref[...].astype(F32), gain_ref[...])[0]


def normalize_kernel(a_ref, b_ref, gain_ref, out_ref):
    rows = [normalized(a_ref, gain_ref), normalized(b_ref, gain_ref)]
    out_ref[...] = jnp.concatenate(rows, axis=0).astype(BF16)


def normalize_rows(a, b, gain):
    shape = shaped((2 * a.shape[0], a.shape[1]), BF16)
    return call(normalize_kernel, shape)(a, b, gain)


def start_kernel(rows_ref, grads_ref, gain_ref, out_ref):
    rows = [normalized(rows_ref, gain_ref), grads_ref[...].astype(F32)]
    out_ref[...] = jnp.concatenate(rows, axis=0).astype(BF16)


def stash_kernel(order_ref, own_ref, other_ref, gain_ref, *out_refs):
    for step, out_ref in enumerate(out_refs):
        slot = order_ref[0, step]
        rows = [normalized(ref.at[slot], gain_ref) for ref in (own_ref, other_ref)]
        out_ref[...] = jnp.concatenate(rows, axis=0).astype(BF16)


def stash_rows(order, own, other, gain):
    steps, size, width = own.shape
    in_vmem = pl.BlockSpec(memory_space=pltpu.VMEM)
    return call(
        stash_kernel,
        [shaped((YS * size, width), BF16)] * steps,
        in_specs=[pl.BlockSpec(memory_space=pltpu.SMEM)] + [in_vmem] * 3,
    )(order, own, other, gain)


def stack_kernel(*refs):
    *piece_refs, out_ref = refs
    rows = [ref[...].astype(F32) for ref in piece_refs]
    out_ref[...] = jnp.concatenate(rows, axis=0).astype(BF16)


def stack_rows(*pieces):
    tokens = sum(piece.shape[0] for piece in pieces)
    return call(stack_kernel, shaped((tokens, pieces[0].shape[1]), BF16))(*pieces)


def split_kernel(size, own_ref, got_ref, keep_ref, up_ref, down_ref, up_two_ref, down_two_ref, far_ref):
    rows = own_ref[...].astype(F32) + got_ref[...].astype(F32)
    keep_ref[...] = rows[:size]
    up_ref[...] = rows[size : 3 * size].astype(BF16)
    down_ref[...] = rows[3 * size : 5 * size].astype(BF16)
    up_two_ref[...] = rows[5 * size : 6 * size].astype(BF16)
    down_two_ref[...] = rows[6 * size : 7 * size].astype(BF16)
    far_ref[...] = rows[7 * size :]


def far_kernel(size, far_ref, up_ref, down_ref, out_ref):
    up, down = up_ref[...].astype(F32), down_ref[...].astype(F32)
    out_ref[...] = (far_ref[...] + up[size:] + down[size:]).astype(BF16)


def scatter_sum(own, got):
    half, width = own.shape
    size, block = half // ZS, width // 3
    outs = [(size, F32), (2 * size, BF16), (2 * size, BF16), (size, BF16), (size, BF16), (size, F32)]
    column = lambda tokens: pl.BlockSpec((tokens, block), lambda i: (0, i))
    keep, up, down, up_two, down_two, far = call(
        functools.partial(split_kernel, size),
        [shaped((tokens, width), dtype) for tokens, dtype in outs],
        grid=(width // block,),
        in_specs=[column(half), column(half)],
        out_specs=[column(tokens) for tokens, _ in outs],
    )(own, got)
    up, down = z_shift(up, 1), z_shift(down, -1)
    up_two, down_two = z_shift(up_two, 2), z_shift(down_two, -2)
    far = call(functools.partial(far_kernel, size), shaped((size, width), BF16))(far, up, down)
    return (keep, up, down, up_two, down_two, z_shift(far, 4))


def total(keep_ref, up_ref, down_ref, up_two_ref, down_two_ref, far_ref):
    size = keep_ref.shape[0]
    up, down = up_ref[...].astype(F32), down_ref[...].astype(F32)
    near = keep_ref[...] + up[:size] + down[:size]
    two = up_two_ref[...].astype(F32) + down_two_ref[...].astype(F32)
    return near + (two + far_ref[...].astype(F32))


def residual_kernel(rows_ref, *refs):
    *addends, out_ref = refs
    out_ref[...] = (rows_ref[...].astype(F32) + total(*addends)).astype(BF16)


def norm_backward(step, order, stash, *arrays):
    in_vmem = pl.BlockSpec(memory_space=pltpu.VMEM)
    return call(
        functools.partial(norm_backward_kernel, step),
        shaped(stash.shape[1:], BF16),
        in_specs=[pl.BlockSpec(memory_space=pltpu.SMEM)] + [in_vmem] * (1 + len(arrays)),
    )(order, stash, *arrays)


def norm_backward_kernel(step, order_ref, stash_ref, grad_ref, gain_ref, *refs):
    *addends, out_ref = refs
    rows = stash_ref[order_ref[0, step]]
    _, scaled, inv_scale = normalize(rows.astype(F32), gain_ref[...])
    d_scaled = total(*addends) * gain_ref[...]
    d_rows = inv_scale * (
        d_scaled
        - jnp.mean(d_scaled, axis=-1, keepdims=True)
        - scaled * jnp.mean(d_scaled * scaled, axis=-1, keepdims=True)
    )
    out_ref[...] = (grad_ref[...].astype(F32) + d_rows).astype(BF16)


def gathered(piece_refs, part, size):
    if part is None:
        return jnp.concatenate([ref[...] for ref in piece_refs], axis=0)
    pieces = [ref[...].astype(F32) for ref in piece_refs]
    span = pieces[0].shape[0]
    blocks = [
        piece[start + part * size : start + (part + 1) * size]
        for piece in pieces
        for start in range(0, piece.shape[0], span)
    ]
    return jnp.concatenate(blocks, axis=0).astype(BF16)


def dot(a, b, dims=(((1,), (0,)), ((), ()))):
    return lax.dot_general(a, b, dims, preferred_element_type=F32)


def probabilities(query, key, visible):
    scores = dot(query, key, TRANSPOSED) * (1.0 / math.sqrt(HD))
    scores = jnp.where(visible, scores, -jnp.inf)
    shifted = jnp.exp(scores - jnp.max(scores, axis=-1, keepdims=True))
    return shifted / jnp.sum(shifted, axis=-1, keepdims=True)


def head_slices(qkv, head):
    inner = qkv.shape[1] // 3
    return [qkv[:, j * inner + head * HD : j * inner + (head + 1) * HD] for j in range(3)]


def add_projections(sums, rows, weight_refs):
    inner = weight_refs[0].shape[0]
    for j, weight_ref in enumerate(weight_refs):
        sums[:, j * inner : (j + 1) * inner] += dot(rows, weight_ref[...], TRANSPOSED)


def forward_kernel(steps_in, pieces, part, *refs):
    piece_refs, (place_ref, *refs) = refs[:pieces], refs[pieces:]
    *weight_refs, proj_ref, visible_ref, own_ref, other_ref, sums, mixed_ref = refs
    step = pl.program_id(0)
    inner = mixed_ref.shape[1]

    @pl.when(step == 0)
    def _():
        sums[...] = jnp.zeros_like(sums)

    @pl.when(step < steps_in)
    def _():
        add_projections(sums, gathered(piece_refs, part, visible_ref.shape[0] // (YS * ZS)), weight_refs)

    @pl.when(step == steps_in - 1)
    def _():
        qkv = dot(place_ref[...], sums[...].astype(BF16)).astype(BF16)
        visible = visible_ref[...] > 0.0
        for head in range(mixed_ref.shape[1] // HD):
            query, key, value = head_slices(qkv, head)
            probs = probabilities(query, key, visible).astype(BF16)
            mixed_ref[:, head * HD : (head + 1) * HD] = dot(probs, value).astype(BF16)

    @pl.when(step >= steps_in)
    def _():
        rows = dot(mixed_ref[...], proj_ref[...])
        half = rows.shape[0] // 2
        own_ref[...] = rows[:half].astype(BF16)
        other_ref[...] = rows[half:].astype(BF16)


def section_call(kernel, pieces, weights, proj, visible, extra, steps, forward):
    tokens, (inner, width) = visible.shape[0], proj.shape
    steps_in, steps_out = steps
    block_in, block_out = width // steps_in, width // steps_out
    first = lambda i: (0, jnp.minimum(i, steps_in - 1))
    second = lambda i: (0, jnp.maximum(i - steps_in, 0))
    whole = lambda i: (0, 0)
    arrays, part, place = pieces
    inputs = [*arrays, place]
    in_specs = [pl.BlockSpec((piece.shape[0], block_in), first) for piece in arrays]
    in_specs.append(pl.BlockSpec(place.shape, whole))
    weight_spec = (block_in, first) if forward else (block_out, second)
    proj_spec = (block_out, second) if forward else (block_in, first)
    in_specs += [pl.BlockSpec((w.shape[0], weight_spec[0]), weight_spec[1]) for w in weights]
    in_specs += [pl.BlockSpec((inner, proj_spec[0]), proj_spec[1])]
    inputs += [*weights, proj, visible, *extra]
    in_specs += [pl.BlockSpec(array.shape, whole) for array in (visible, *extra)]
    scratch = [(3 * inner, F32), (inner, BF16)] if forward else [(inner, F32), (3 * inner, BF16)]
    return call(
        functools.partial(kernel, steps_in, len(arrays), part),
        [shaped((tokens // 2, width), BF16)] * 2,
        flops=8 * tokens * inner * width,
        moved=24 * inner * width + 8 * tokens * width,
        grid=(steps_in + steps_out,),
        in_specs=in_specs,
        out_specs=[pl.BlockSpec((tokens // 2, block_out), second)] * 2,
        scratch_shapes=[pltpu.VMEM((tokens, columns), dtype) for columns, dtype in scratch],
    )(*inputs)


def forward_section(pieces, weights, proj, visible):
    return section_call(
        forward_kernel, pieces, weights, proj, visible, (), (4, 3), True
    )


def qkv_kernel(rows_ref, place_ref, *refs):
    *weight_refs, out_ref, sums = refs
    step = pl.program_id(0)

    @pl.when(step == 0)
    def _():
        sums[...] = jnp.zeros_like(sums)

    add_projections(sums, rows_ref[...], weight_refs)

    @pl.when(step == pl.num_programs(0) - 1)
    def _():
        out_ref[...] = dot(place_ref[...], sums[...].astype(BF16)).astype(BF16)


def qkv_section(rows, place, weights):
    tokens, width = rows.shape
    columns = sum(w.shape[0] for w in weights)
    blocks = 4
    block = width // blocks
    column = lambda i: (0, i)
    whole = lambda i: (0, 0)
    return call(
        qkv_kernel,
        shaped((tokens, columns), BF16),
        flops=2 * tokens * columns * width,
        moved=4 * columns * width,
        grid=(blocks,),
        in_specs=[pl.BlockSpec((tokens, block), column), pl.BlockSpec(place.shape, whole)]
        + [pl.BlockSpec((w.shape[0], block), column) for w in weights],
        out_specs=pl.BlockSpec((tokens, columns), whole),
        scratch_shapes=[pltpu.VMEM((tokens, columns), F32)],
    )(rows, place, *weights)


def backward_kernel(steps_in, pieces, part, *refs):
    piece_refs, (place_ref, *refs) = refs[:pieces], refs[pieces:]
    *weight_refs, proj_ref, visible_ref, qkv_ref, own_ref, other_ref, sums, d_qkv_ref = refs
    step = pl.program_id(0)

    @pl.when(step == 0)
    def _():
        sums[...] = jnp.zeros_like(sums)

    @pl.when(step < steps_in)
    def _():
        sums[...] += dot(gathered(piece_refs, part, visible_ref.shape[0] // (YS * ZS)), proj_ref[...], TRANSPOSED)

    @pl.when(step == steps_in - 1)
    def _():
        d_mixed = dot(place_ref[...], sums[...].astype(BF16)).astype(BF16)
        inner = d_mixed.shape[1]
        visible = visible_ref[...] > 0.0
        qkv = qkv_ref[...]
        for head in range(inner // HD):
            query, key, value = head_slices(qkv, head)
            mixed = d_mixed[:, head * HD : (head + 1) * HD]
            probs = probabilities(query, key, visible)
            d_probs = dot(mixed, value, TRANSPOSED)
            probs_turned = probs.T.astype(BF16)
            d_scores = (
                probs
                * (d_probs - jnp.sum(d_probs * probs, axis=-1, keepdims=True))
                * (1.0 / math.sqrt(HD))
            )
            parts = (
                dot(d_scores.astype(BF16), key),
                dot(d_scores.T.astype(BF16), query),
                dot(probs_turned, mixed),
            )
            for j, part in enumerate(parts):
                place = j * inner + head * HD
                d_qkv_ref[:, place : place + HD] = part.astype(BF16)

    @pl.when(step >= steps_in)
    def _():
        inner = weight_refs[0].shape[0]
        rows = sum(
            dot(d_qkv_ref[:, j * inner : (j + 1) * inner], weight_ref[...])
            for j, weight_ref in enumerate(weight_refs)
        )
        half = rows.shape[0] // 2
        own_ref[...] = rows[:half].astype(BF16)
        other_ref[...] = rows[half:].astype(BF16)


def backward_section(pieces, weights, proj, visible, qkv):
    return section_call(
        backward_kernel, pieces, weights, proj, visible, (qkv,), (3, 4), False
    )


def on_device(
    new_inputs,
    new_grads,
    forward_state,
    backward_state,
    stashed,
    new_docs,
    state_docs,
    stash_docs,
    stash_order,
    norm_gain,
    qkv_weight,
    out_weight,
):
    proj = out_weight[0]
    pipe_index = lax.axis_index("pipe")
    last_pipe = lax.axis_size("pipe") - 1
    size = forward_state.shape[1]
    tokens = size * YS * ZS
    y_index, z_index = lax.axis_index("y"), lax.axis_index("z")

    def tokens_of(blocks):
        starts = [((y_index + y) % YS * ZS + (z_index + z + ZS) % ZS) * size for y, z in blocks]
        return jnp.concatenate([start + lax.iota(jnp.int32, size) for start in starts])

    positions = tokens_of([(y, z) for y in range(YS) for z in Z_ORDER])

    def place_of(order):
        return (positions[:, None] == order[None, :]).astype(BF16)

    ring_place = place_of(tokens_of([(y, z) for y in range(YS) for z in EARLY + LATE]))
    pairs_place = place_of(tokens_of([(y, z) for z in Z_ORDER for y in range(YS)]))
    by_z = [z - z_index for z in range(ZS)]
    stash_place = place_of(tokens_of([(y, z) for z in by_z for y in range(YS)]))
    chosen = positions[:, None] == lax.iota(jnp.int32, tokens)[None, :]
    before = positions[:, None] >= positions[None, :]

    def visible_from(ids):
        ids = jnp.sum(jnp.where(chosen, ids[None, :], 0), axis=1)
        return jnp.where(before & (ids[:, None] == ids[None, :]), 1.0, 0.0).astype(F32)

    stash, stored_visible = stashed[0], []
    for phase in range(STEPS):
        ids = lax.dynamic_index_in_dim(stash_docs[0], stash_order[0, phase], 0, keepdims=False)
        stored_visible.append(visible_from(ids))
    visible = [visible_from(state_docs[0]), None]

    rows, grads = forward_state[0], backward_state[0]
    size, width = rows.shape
    start = call(start_kernel, shaped((2 * size, width), BF16))(rows, grads, norm_gain)
    stash_swapped = y_swap(after(stash, start))
    stash_pieces = []

    def stash_ready(arrived):
        other = after(stash_swapped, arrived)
        stash_pieces.extend(stash_rows(stash_order, stash, other, norm_gain))
        return stash_pieces[0]

    arrays = gather_z_first(start, stash_ready)
    stash_pieces = [lax.all_gather(piece, "z", axis=0, tiled=True) for piece in stash_pieces]
    weight = jnp.transpose(after(qkv_weight, *arrays[:ZS])[0], (1, 2, 0))
    weights = [weight.reshape(-1, weight.shape[2])]
    pieces, grad_pieces = (arrays, 0, ring_place), (arrays, 1, ring_place)

    qkv_stash = [None, None]
    for phase in range(STEPS):
        own, other = forward_section(pieces, weights, proj, visible[phase])
        got = y_swap(other)
        if phase == 0:
            qkv_stash[0] = qkv_section(after(stash_pieces[0], own), stash_place, weights)
            ids = from_behind(after(state_docs[0], own), 1)
            visible[1] = visible_from(jnp.where(pipe_index == 0, new_docs[0], ids))
            entering = (new_inputs[0], y_swap(after(new_inputs[0], own)))
        arrays, part, place = grad_pieces
        grad_pieces = ([after(arrays[0], own)] + arrays[1:], part, place)
        d_own, d_other = backward_section(
            grad_pieces, weights, proj, stored_visible[phase], qkv_stash[phase]
        )
        sums = scatter_sum(own, after(got, d_own))
        d_got = y_swap(d_other)
        if phase == 0:
            qkv_stash[1] = qkv_section(after(stash_pieces[1], d_own), stash_place, weights)
            d_got = after(d_got, qkv_stash[1])
        if phase == 0:
            sums = (after(sums[0], d_got), *sums[1:])
        d_sums = scatter_sum(d_own, d_got)
        rows_next = call(residual_kernel, shaped(rows.shape, BF16))(rows, *sums)
        grads_next = norm_backward(phase, stash_order, stash, grads, norm_gain, *d_sums)
        if phase + 1 < STEPS:
            at_end, at_start = pipe_index == last_pipe, pipe_index == 0
            came = (from_behind(rows_next, 1), from_behind_swapped(rows_next, 1))
            came = [jnp.where(at_start, new, old) for new, old in zip(entering, came)]
            rows = came[0]
            arrays = gather_y_first(normalize_rows(*came, norm_gain))
            grads = jnp.where(at_end, new_grads[0], from_behind(grads_next, -1))
            grad_pieces = (gather_z_first(grads), 0, ring_place)
            pieces = (arrays, None, pairs_place)
    return (rows_next[None], grads_next[None])


def solution(mesh):
    split = Mesh(mesh.devices.reshape(-1, YS, ZS), ("pipe", "y", "z"))
    tensor = ("y", "z")
    return jax.shard_map(
        on_device,
        mesh=split,
        in_specs=(
            P(None, tensor, None),
            P(None, tensor, None),
            P("pipe", tensor, None),
            P("pipe", tensor, None),
            P("pipe", None, tensor, None),
            P(),
            P("pipe", None),
            P("pipe", None, None),
            P("pipe", None),
            P("pipe", None),
            P("pipe", None, None, tensor),
            P("pipe", tensor, None),
        ),
        out_specs=(P("pipe", tensor, None), P("pipe", tensor, None)),
        check_vma=False,
    )
```
